32 devices in a mesh: row: 8 (over z, y), col: 4 (over x, core).
Axes of the slice: x: 2, y: 2, z: 4, core: 2. Of those that a mesh axis runs over, the one named last changes fastest.
Arguments:
- queries: float32 [16384, 256], P(('row', 'col')), may hold values from -1 to 1
- passages: float32 [16384, 256], P(('col', 'row')), may hold values from -1 to 1
- mean_cost: float32 [1], replicated, may hold values from 1 to 3
Outputs:
- row_potential: float32 [16384], P('row')
- col_potential: float32 [16384], P('col')
The draws below stay inside these ranges and needn't reach their ends.
All inputs are finite; a program needn't handle non-finite values.
Results may differ from the reference program's by a relative error of at most 0.0003.
Values sent between devices are 32-bit elements; how exact they have to be, the bound alone decides.
A program may use at most 256 MiB of HBM per device.

```python
import math
import jax
import jax.numpy as jnp
from jax import lax

D = 256
ITERS = 3
QUERIES = 16384
PASSAGES = 16384


def shared_pair(key):
    subkeys = [jax.random.fold_in(key, 101 + offset) for offset in range(6)]
    passage_base = jax.random.truncated_normal(subkeys[0], -4.0, 4.0, (PASSAGES, D), jnp.float32) * D ** (-0.5)
    query_base = jax.random.truncated_normal(subkeys[1], -4.0, 4.0, (QUERIES, D), jnp.float32) * D ** (-0.5)
    lower_log = math.log(0.5)
    upper_log = math.log(1.6)
    passage_scale = jnp.exp(jax.random.uniform(subkeys[2], (PASSAGES, 1), jnp.float32, lower_log, upper_log))
    query_scale = jnp.exp(jax.random.uniform(subkeys[3], (QUERIES, 1), jnp.float32, lower_log, upper_log))
    passages = passage_base * passage_scale
    queries = query_base * query_scale
    distant = query_base[8:16] + 6.0 * D ** (-0.5)
    queries = jnp.concatenate([queries[0:8], distant, queries[16:]], axis=0)
    return (queries, passages)


def draw_queries(key, part):
    return shared_pair(key)[0]


def draw_passages(key, part):
    return shared_pair(key)[1]


def setup_inputs(seed: int = 0) -> dict:
    splits = jax.random.split(jax.random.key(seed), 4)
    queries = draw_queries(jax.random.fold_in(splits[3], 71), 0)
    passages = draw_passages(jax.random.fold_in(splits[3], 71), 0)
    mean_cost = jnp.clip(jax.random.uniform(splits[2], (1,), jnp.float32, 1.0, 3.0), 1.0, 3.0)
    return dict(queries=queries, passages=passages, mean_cost=mean_cost)


def pair_costs(left, right):
    left_norms = jnp.sum(left * left, axis=1)
    right_norms = jnp.sum(right * right, axis=1)
    inner = jnp.dot(left, right.T, precision=lax.Precision.HIGHEST, preferred_element_type=jnp.float32)
    return (left_norms[:, None] + right_norms[None, :]) - 2.0 * inner


def block_logsum(left, right, potential, entropy_scale):
    width = math.gcd(left.shape[0], 512)
    blocks = left.reshape(left.shape[0] // width, width, left.shape[1])

    def one_block(block_rows):
        scores = (potential[None, :] - pair_costs(block_rows, right)) / entropy_scale
        peak = jnp.max(scores, axis=1)
        return peak + jnp.log(jnp.sum(jnp.exp(scores - peak[:, None]), axis=1))

    return lax.map(one_block, blocks).reshape(-1)


def reference(queries, passages, mean_cost):
    entropy_scale = 0.1 * mean_cost[0]
    col_potential = jnp.zeros((PASSAGES,), jnp.float32)
    row_potential = jnp.zeros((QUERIES,), jnp.float32)
    for repeat in range(ITERS):
        row_potential = -entropy_scale * math.log(QUERIES) - entropy_scale * block_logsum(queries, passages, col_potential, entropy_scale)
        col_potential = -entropy_scale * math.log(PASSAGES) - entropy_scale * block_logsum(passages, queries, row_potential, entropy_scale)
    return row_potential, col_potential
```

```python
import functools
import math

import jax
import jax.numpy as jnp
from jax import lax
from jax.experimental import pallas as pl
from jax.experimental.pallas import tpu as pltpu
from jax.sharding import PartitionSpec as P

ITERS = 3
LOG2E = 1.4426950408889634
LOW = -3.0e38
LANES = 128
MESH = pl.DeviceIdType.MESH


def tree(op, values):
    values = list(values)
    while len(values) > 1:
        values = [
            op(values[i], values[i + 1]) if i + 1 < len(values) else values[i]
            for i in range(0, len(values), 2)
        ]
    return values[0]


def online(m, s, z):
    new = jnp.maximum(m, tree(jnp.maximum, z))
    return new, s * jnp.exp2(m - new) + tree(jnp.add, [jnp.exp2(v - new) for v in z])


def kernel(
    nr, nc, log_q, log_p,
    mc_ref, q_ref, p_ref, f_out, g_out,
    tile, qbuf, pbuf, q3, p3, qn, pn, g8, fb, m_rows, s_rows, m_cols, s_cols, rbuf, cbuf,
    q_send, q_recv, p_send, p_recv, r_send, r_recv, c_send, c_recv,
):
    row, col = lax.axis_index("row"), lax.axis_index("col")
    qb, depth = q_ref.shape
    pb = p_ref.shape[0]
    rows, cols = qb * nc, pb * nr
    nx = nc // 2
    core = lax.rem(col, 2)
    sibling = col + 1 - 2 * core

    barrier = pltpu.get_barrier_semaphore()
    for d in range(1, nr):
        pl.semaphore_signal(
            barrier, inc=1, device_id=(lax.rem(row + d, nr), col), device_id_type=MESH
        )
    for d in range(1, nc):
        pl.semaphore_signal(
            barrier, inc=1, device_id=(row, lax.rem(col + d, nc)), device_id_type=MESH
        )
    pl.semaphore_wait(barrier, nr + nc - 2)

    def remote(src, dst, send, recv, device):
        return pltpu.make_async_remote_copy(
            src_ref=src, dst_ref=dst, send_sem=send, recv_sem=recv,
            device_id=device, device_id_type=MESH,
        )

    half = nr // 2

    def at(pos):
        pos = lax.rem(pos + 2 * nr, nr)
        y = pos // half
        z = pos * (1 - y) + (nr - 1 - pos) * y
        return 2 * z + y

    row_y = lax.rem(row, 2)
    row_z = row // 2
    pos = row_z + row_y * (nr - 1 - 2 * row_z)
    ahead, behind = at(pos + 1), at(pos - 1)

    def ring(step):
        a, b = at(pos - (step - 1)), at(pos + (step - 1))
        if step == half:
            h = pb // 2
            parts = (pl.ds(0, h), pl.ds(h, h))
        else:
            parts = (pl.ds(0, pb), pl.ds(0, pb))
        out = []
        for way, (owner, device) in enumerate(((a, ahead), (b, behind))):
            src = p_ref.at[parts[way]] if step == 1 else pbuf.at[owner, parts[way]]
            out.append(
                remote(
                    src, pbuf.at[owner, parts[way]],
                    p_send.at[way, step], p_recv.at[way, step], (device, col),
                )
            )
        return out

    steps = {1: ring(1)}
    for c in steps[1]:
        c.start()

    cross, passed = [], []
    for d in range(1, nx):
        cross.append(
            remote(
                q_ref, qbuf.at[col], q_send.at[d], q_recv.at[d],
                (row, lax.rem(col + 2 * d, nc)),
            )
        )
    for c in cross:
        c.start()
    own = remote(q_ref, qbuf.at[col], q_send.at[0], q_recv.at[0], (row, sibling))
    own.start()

    kappa = (10.0 * LOG2E) / jnp.full((8, LANES), mc_ref[0], jnp.float32)
    kappa1 = kappa[0:1, :]

    def norms(x):
        sq = x * x
        total = sq[:, 0:LANES]
        for k in range(1, depth // LANES):
            total = total + sq[:, k * LANES : (k + 1) * LANES]
        return jnp.sum(total.T, axis=0, keepdims=True)

    def split_q(block, ref):
        def body(i, _):
            x = ref[pl.ds(pl.multiple_of(i * LANES, LANES), LANES), :]
            qn[block, pl.ds(i, 1), :] = norms(x)
            for k in range(depth // LANES):
                v = x[:, k * LANES : (k + 1) * LANES] * (2.0 * kappa1)
                hi = v.astype(jnp.bfloat16)
                lo = (v - hi.astype(jnp.float32)).astype(jnp.bfloat16)
                at_row = pl.ds(pl.multiple_of(block * qb + i * LANES, LANES), LANES)
                q3[at_row, k * LANES : (k + 1) * LANES] = hi
                q3[at_row, depth + k * LANES : depth + (k + 1) * LANES] = hi
                q3[at_row, 2 * depth + k * LANES : 2 * depth + (k + 1) * LANES] = lo
            return 0

        lax.fori_loop(0, qb // LANES, body, 0)

    m_rows[...] = jnp.full(m_rows.shape, LOW, jnp.float32)
    s_rows[...] = jnp.zeros(s_rows.shape, jnp.float32)

    def work(block, ref, start, size):
        base = pl.multiple_of(block * pb + start, LANES)
        for i in range(size // LANES):
            at_row = start + i * LANES
            x = ref[at_row : at_row + LANES, :]
            norm = norms(x)
            pn[block, start // LANES + i : start // LANES + i + 1, :] = norm
            g8[:, pl.ds(pl.multiple_of(base + i * LANES, LANES), LANES)] = jnp.broadcast_to(
                -norm * kappa1, (8, LANES)
            )
            hi = x.astype(jnp.bfloat16)
            lo = (x - hi.astype(jnp.float32)).astype(jnp.bfloat16)
            p3[i * LANES : (i + 1) * LANES, 0:depth] = hi
            p3[i * LANES : (i + 1) * LANES, depth : 2 * depth] = lo
            p3[i * LANES : (i + 1) * LANES, 2 * depth : 3 * depth] = hi

        def product(i, _):
            at_row = pl.ds(pl.multiple_of(i * 512, 512), 512)
            tile[at_row, pl.ds(base, size)] = lax.dot_general(
                q3[at_row, :], p3[0:size, :], (((1,), (1,)), ((), ())),
                preferred_element_type=jnp.float32,
            )
            return 0

        lax.fori_loop(0, rows // 512, product, 0)
        width = size // LANES

        def first(i, _):
            g = [g8[:, pl.ds(pl.multiple_of(base + k * LANES, LANES), LANES)] for k in range(width)]
            for r in range(8):
                at_row = pl.ds(pl.multiple_of(i * 64 + r * 8, 8), 8)
                z = [
                    tile[at_row, pl.ds(pl.multiple_of(base + k * LANES, LANES), LANES)] + g[k]
                    for k in range(width)
                ]
                m_rows[at_row, :], s_rows[at_row, :] = online(m_rows[at_row, :], s_rows[at_row, :], z)
            return 0

        lax.fori_loop(0, rows // 64, first, 0)

    split_q(col, q_ref)
    for d, c in enumerate(cross, 1):
        c.wait_recv()
        source = lax.rem(col - 2 * d + nc, nc)
        fwd = remote(
            qbuf.at[source], qbuf.at[source], q_send.at[nx + d - 1], q_recv.at[nx + d - 1],
            (row, sibling),
        )
        fwd.start()
        passed.append(fwd)
        split_q(source, qbuf.at[source])
    own.wait_recv()
    split_q(sibling, qbuf.at[sibling])
    for d, c in enumerate(passed, 1):
        c.wait_recv()
        source = lax.rem(sibling - 2 * d + nc, nc)
        split_q(source, qbuf.at[source])

    for step in range(1, half + 1):
        if step == 1:
            work(row, p_ref, 0, pb)
        for c in steps[step]:
            c.wait_recv()
        if step < half:
            steps[step + 1] = ring(step + 1)
            for c in steps[step + 1]:
                c.start()
            for owner in (at(pos - step), at(pos + step)):
                work(owner, pbuf.at[owner], 0, pb)
        else:
            owner = at(pos + half)
            work(owner, pbuf.at[owner], 0, pb)

    def exchange(buf, t, me, n, send, recv, device):
        sent = []
        for d in range(1, n):
            c = remote(
                buf.at[t, me], buf.at[t, me], send.at[t, d], recv.at[t, d],
                device(lax.rem(me + d, n)),
            )
            c.start()
            sent.append(c)
        for c in sent:
            c.wait_recv()
        parts = [buf[t, i] for i in range(n)]
        peak = tree(jnp.maximum, parts)
        total = jnp.exp2(parts[0] - peak)
        for part in parts[1:]:
            total = total + jnp.exp2(part - peak)
        for c in sent:
            c.wait_send()
        return peak + jnp.log2(total)

    def row_pass():
        wide = cols // LANES
        chunk = min(16, wide)

        def body(i, _):
            pair = []
            for h in range(2):
                pair.append(
                    (jnp.full((8, LANES), LOW, jnp.float32), jnp.zeros((8, LANES), jnp.float32))
                )
            for k0 in range(0, wide, chunk):
                for h in range(2):
                    at_row = pl.ds(pl.multiple_of(i * 16 + h * 8, 8), 8)
                    z = [
                        tile[at_row, k * LANES : (k + 1) * LANES] + g8[:, k * LANES : (k + 1) * LANES]
                        for k in range(k0, k0 + chunk)
                    ]
                    pair[h] = online(*pair[h], z)
            for h in range(2):
                at_row = pl.ds(pl.multiple_of(i * 16 + h * 8, 8), 8)
                m_rows[at_row, :], s_rows[at_row, :] = pair[h]
            return 0

        lax.fori_loop(0, rows // 16, body, 0)

    def col_pass():
        def strip(k, _):
            lanes = [
                pl.ds(pl.multiple_of(k * 2 * LANES + h * LANES, LANES), LANES) for h in range(2)
            ]

            def body(c, carry):
                f = [fb[pl.ds(pl.multiple_of(c * 128 + r * 8, 8), 8), :] for r in range(16)]
                out = []
                for h in range(2):
                    z = [
                        tile[pl.ds(pl.multiple_of(c * 128 + r * 8, 8), 8), lanes[h]] + f[r]
                        for r in range(16)
                    ]
                    out.extend(online(carry[2 * h], carry[2 * h + 1], z))
                return tuple(out)

            low = jnp.full((8, LANES), LOW, jnp.float32)
            zero = jnp.zeros((8, LANES), jnp.float32)
            done = lax.fori_loop(0, rows // 128, body, (low, zero, low, zero))
            for h in range(2):
                m_cols[:, lanes[h]] = done[2 * h]
                s_cols[:, lanes[h]] = done[2 * h + 1]
            return 0

        lax.fori_loop(0, cols // (2 * LANES), strip, 0)

    for t in range(ITERS):
        if t > 0:
            row_pass()
        for b in range(rows // LANES):
            here = slice(b * LANES, (b + 1) * LANES)
            m, s = m_rows[here, :].T, s_rows[here, :].T
            peak = jnp.max(m, axis=0, keepdims=True)
            total = jnp.sum(s * jnp.exp2(m - peak), axis=0, keepdims=True)
            rbuf[t, col, b : b + 1, :] = peak + jnp.log2(total)
        f = -log_q - exchange(rbuf, t, col, nc, r_send, r_recv, lambda i: (row, i))
        for b in range(rows // LANES):
            fb[b * LANES : (b + 1) * LANES, :] = jnp.broadcast_to(
                f[b : b + 1, :], (LANES, LANES)
            ).T
        if t == ITERS - 1:
            per = qb // LANES
            for b in range(nc):
                here = slice(b * per, (b + 1) * per)
                f_out[here, :] = f[here, :] / kappa1 + qn[b]
        col_pass()
        for k in range(cols // LANES):
            here = slice(k * LANES, (k + 1) * LANES)
            m, s = m_cols[:, here], s_cols[:, here]
            peak = jnp.max(m, axis=0, keepdims=True)
            total = jnp.sum(s * jnp.exp2(m - peak), axis=0, keepdims=True)
            cbuf[t, row, k : k + 1, :] = peak + jnp.log2(total)
        g = -log_p - exchange(cbuf, t, row, nr, c_send, c_recv, lambda i: (i, col))
        if t < ITERS - 1:
            for k in range(cols // LANES):
                g8[:, k * LANES : (k + 1) * LANES] = jnp.broadcast_to(g[k : k + 1, :], (8, LANES))
        else:
            per = pb // LANES
            for b in range(nr):
                here = slice(b * per, (b + 1) * per)
                g_out[here, :] = g[here, :] / kappa1 + pn[b]

    for c in cross + [own] + passed:
        c.wait_send()
    for step in range(1, half + 1):
        for c in steps[step]:
            c.wait_send()


def per_device(nr, nc, queries, passages, mean_cost):
    qb, depth = queries.shape
    pb = passages.shape[0]
    rows, cols = qb * nc, pb * nr
    f32, bf16 = jnp.float32, jnp.bfloat16
    dma = pltpu.SemaphoreType.DMA
    vmem = pl.BlockSpec(memory_space=pltpu.VMEM)
    f, g = pl.pallas_call(
        functools.partial(
            kernel, nr, nc, math.log2(qb * nr * nc), math.log2(pb * nr * nc)
        ),
        out_shape=(
            jax.ShapeDtypeStruct((rows // LANES, LANES), f32),
            jax.ShapeDtypeStruct((cols // LANES, LANES), f32),
        ),
        in_specs=[pl.BlockSpec(memory_space=pltpu.SMEM), vmem, vmem],
        out_specs=(vmem, vmem),
        scratch_shapes=[
            pltpu.VMEM((rows, cols), f32),
            pltpu.VMEM((nc, qb, depth), f32),
            pltpu.VMEM((nr, pb, depth), f32),
            pltpu.VMEM((rows, 3 * depth), bf16),
            pltpu.VMEM((pb, 3 * depth), bf16),
            pltpu.VMEM((nc, qb // LANES, LANES), f32),
            pltpu.VMEM((nr, pb // LANES, LANES), f32),
            pltpu.VMEM((8, cols), f32),
            pltpu.VMEM((rows, LANES), f32),
            pltpu.VMEM((rows, LANES), f32),
            pltpu.VMEM((rows, LANES), f32),
            pltpu.VMEM((8, cols), f32),
            pltpu.VMEM((8, cols), f32),
            pltpu.VMEM((ITERS, nc, rows // LANES, LANES), f32),
            pltpu.VMEM((ITERS, nr, cols // LANES, LANES), f32),
            dma((nc,)), dma((nc,)),
            dma((2, nr // 2 + 1)), dma((2, nr // 2 + 1)),
            dma((ITERS, nc)), dma((ITERS, nc)),
            dma((ITERS, nr)), dma((ITERS, nr)),
        ],
        compiler_params=pltpu.CompilerParams(
            collective_id=0, has_side_effects=True, vmem_limit_bytes=60 * 1024 * 1024
        ),
        cost_estimate=pl.CostEstimate(
            flops=6 * rows * cols * depth,
            bytes_accessed=4 * depth * (qb + pb),
            transcendentals=2 * ITERS * rows * cols,
        ),
    )(mean_cost, queries, passages)
    return f.reshape(rows), g.reshape(cols)


def solution(mesh):
    nr, nc = mesh.shape["row"], mesh.shape["col"]
    placed = (P(("row", "col"), None), P(("col", "row"), None), P())
    return jax.shard_map(
        functools.partial(per_device, nr, nc),
        mesh=mesh, in_specs=placed, out_specs=(P("row"), P("col")), check_vma=False,
    )
```

```python
import functools
import math

import jax
import jax.numpy as jnp
from jax import lax
from jax.experimental import pallas as pl
from jax.experimental.pallas import tpu as pltpu
from jax.sharding import PartitionSpec as P

ITERS = 3
LOG2E = 1.4426950408889634
LOW = -3.0e38
LANES = 128
MESH = pl.DeviceIdType.MESH


def tree(op, values):
    values = list(values)
    while len(values) > 1:
        values = [
            op(values[i], values[i + 1]) if i + 1 < len(values) else values[i]
            for i in range(0, len(values), 2)
        ]
    return values[0]


def online(m, s, z):
    new = jnp.maximum(m, tree(jnp.maximum, z))
    return new, s * jnp.exp2(m - new) + tree(jnp.add, [jnp.exp2(v - new) for v in z])


def kernel(
    nr, nc, log_q, log_p,
    mc_ref, q_ref, p_ref, f_out, g_out,
    tile, qbuf, pbuf, q3, p3, qn, pn, g8, fb, m_rows, s_rows, m_cols, s_cols, rbuf, cbuf,
    q_send, q_recv, p_send, p_recv, r_send, r_recv, c_send, c_recv,
):
    row, col = lax.axis_index("row"), lax.axis_index("col")
    qb, depth = q_ref.shape
    pb = p_ref.shape[0]
    rows, cols = qb * nc, pb * nr
    nx = nc // 2
    core = lax.rem(col, 2)
    sibling = col + 1 - 2 * core

    barrier = pltpu.get_barrier_semaphore()
    for d in range(1, nr):
        pl.semaphore_signal(
            barrier, inc=1, device_id=(lax.rem(row + d, nr), col), device_id_type=MESH
        )
    for d in range(1, nc):
        pl.semaphore_signal(
            barrier, inc=1, device_id=(row, lax.rem(col + d, nc)), device_id_type=MESH
        )
    pl.semaphore_wait(barrier, nr + nc - 2)

    def remote(src, dst, send, recv, device):
        return pltpu.make_async_remote_copy(
            src_ref=src, dst_ref=dst, send_sem=send, recv_sem=recv,
            device_id=device, device_id_type=MESH,
        )

    half = nr // 2

    def at(pos):
        pos = lax.rem(pos + 2 * nr, nr)
        y = pos // half
        z = pos * (1 - y) + (nr - 1 - pos) * y
        return 2 * z + y

    row_y = lax.rem(row, 2)
    row_z = row // 2
    pos = row_z + row_y * (nr - 1 - 2 * row_z)
    ahead, behind = at(pos + 1), at(pos - 1)

    def ring(step):
        a, b = at(pos - (step - 1)), at(pos + (step - 1))
        if step == half:
            h = pb // 2
            parts = (pl.ds(0, h), pl.ds(h, h))
        else:
            parts = (pl.ds(0, pb), pl.ds(0, pb))
        out = []
        for way, (owner, device) in enumerate(((a, ahead), (b, behind))):
            src = p_ref.at[parts[way]] if step == 1 else pbuf.at[owner, parts[way]]
            out.append(
                remote(
                    src, pbuf.at[owner, parts[way]],
                    p_send.at[way, step], p_recv.at[way, step], (device, col),
                )
            )
        return out

    steps = {1: ring(1)}
    for c in steps[1]:
        c.start()

    cross, passed = [], []
    for d in range(1, nx):
        cross.append(
            remote(
                q_ref, qbuf.at[col], q_send.at[d], q_recv.at[d],
                (row, lax.rem(col + 2 * d, nc)),
            )
        )
    for c in cross:
        c.start()
    own = remote(q_ref, qbuf.at[col], q_send.at[0], q_recv.at[0], (row, sibling))
    own.start()

    kappa = (10.0 * LOG2E) / jnp.full((8, LANES), mc_ref[0], jnp.float32)
    kappa1 = kappa[0:1, :]

    def norms(x):
        sq = x * x
        total = sq[:, 0:LANES]
        for k in range(1, depth // LANES):
            total = total + sq[:, k * LANES : (k + 1) * LANES]
        return jnp.sum(total.T, axis=0, keepdims=True)

    def split_q(block, ref):
        def body(i, _):
            x = ref[pl.ds(pl.multiple_of(i * LANES, LANES), LANES), :]
            qn[block, pl.ds(i, 1), :] = norms(x)
            for k in range(depth // LANES):
                v = x[:, k * LANES : (k + 1) * LANES] * (2.0 * kappa1)
                hi = v.astype(jnp.bfloat16)
                lo = (v - hi.astype(jnp.float32)).astype(jnp.bfloat16)
                at_row = pl.ds(pl.multiple_of(block * qb + i * LANES, LANES), LANES)
                q3[at_row, k * LANES : (k + 1) * LANES] = hi
                q3[at_row, depth + k * LANES : depth + (k + 1) * LANES] = hi
                q3[at_row, 2 * depth + k * LANES : 2 * depth + (k + 1) * LANES] = lo
            return 0

        lax.fori_loop(0, qb // LANES, body, 0)

    m_rows[...] = jnp.full(m_rows.shape, LOW, jnp.float32)
    s_rows[...] = jnp.zeros(s_rows.shape, jnp.float32)

    wide = pb // LANES

    def prepare(block, ref):
        base = pl.multiple_of(block * pb, LANES)
        for i in range(wide):
            x = ref[i * LANES : (i + 1) * LANES, :]
            norm = norms(x)
            pn[block, i : i + 1, :] = norm
            g8[:, pl.ds(pl.multiple_of(base + i * LANES, LANES), LANES)] = jnp.broadcast_to(
                -norm * kappa1, (8, LANES)
            )
            hi = x.astype(jnp.bfloat16)
            lo = (x - hi.astype(jnp.float32)).astype(jnp.bfloat16)
            p3[i * LANES : (i + 1) * LANES, 0:depth] = hi
            p3[i * LANES : (i + 1) * LANES, depth : 2 * depth] = lo
            p3[i * LANES : (i + 1) * LANES, 2 * depth : 3 * depth] = hi

    def work(block, q_block):
        base = pl.multiple_of(block * pb, LANES)
        top = pl.multiple_of(q_block * qb, qb)
        tile[pl.ds(top, qb), pl.ds(base, pb)] = lax.dot_general(
            q3[pl.ds(top, qb), :], p3[...], (((1,), (1,)), ((), ())),
            preferred_element_type=jnp.float32,
        )

        def first(i, _):
            g = [g8[:, pl.ds(pl.multiple_of(base + k * LANES, LANES), LANES)] for k in range(wide)]
            for r in range(16):
                at_row = pl.ds(pl.multiple_of(top + i * 128 + r * 8, 8), 8)
                z = [
                    tile[at_row, pl.ds(pl.multiple_of(base + k * LANES, LANES), LANES)] + g[k]
                    for k in range(wide)
                ]
                m_rows[at_row, :], s_rows[at_row, :] = online(m_rows[at_row, :], s_rows[at_row, :], z)
            return 0

        lax.fori_loop(0, qb // 128, first, 0)

    sent = []

    def send_out(buf, t, h, me, n, send, recv, device):
        size = buf.shape[2] // 2
        half_part = buf.at[t, me, pl.ds(h * size, size)]
        copies = []
        for d in range(1, n):
            c = remote(
                half_part, half_part, send.at[t, h, d], recv.at[t, h, d], device(lax.rem(me + d, n))
            )
            c.start()
            copies.append(c)
        sent.extend(copies)
        return copies

    def take_in(buf, t, h, n, copies):
        for c in copies:
            c.wait_recv()
        size = buf.shape[2] // 2
        parts = [buf[t, i, h * size : (h + 1) * size, :] for i in range(n)]
        peak = tree(jnp.maximum, parts)
        total = jnp.exp2(parts[0] - peak)
        for part in parts[1:]:
            total = total + jnp.exp2(part - peak)
        return peak + jnp.log2(total)

    h_rows, h_cols = rows // 2, cols // 2

    def send_rows(t, h):
        for b in range(h * h_rows // LANES, (h + 1) * h_rows // LANES):
            here = slice(b * LANES, (b + 1) * LANES)
            m, s = m_rows[here, :].T, s_rows[here, :].T
            peak = jnp.max(m, axis=0, keepdims=True)
            total = jnp.sum(s * jnp.exp2(m - peak), axis=0, keepdims=True)
            rbuf[t, col, b : b + 1, :] = peak + jnp.log2(total)
        return send_out(rbuf, t, h, col, nc, r_send, r_recv, lambda i: (row, i))

    def take_rows(t, h, copies):
        f = -log_q - take_in(rbuf, t, h, nc, copies)
        for b in range(h_rows // LANES):
            at_row = h * h_rows + b * LANES
            fb[at_row : at_row + LANES, :] = jnp.broadcast_to(f[b : b + 1, :], (LANES, LANES)).T
        if t == ITERS - 1:
            per = qb // LANES
            for b in range(nc // 2):
                block = h * (nc // 2) + b
                f_out[block * per : (block + 1) * per, :] = (
                    f[b * per : (b + 1) * per, :] / kappa1 + qn[block]
                )

    def send_cols(t, h):
        for k in range(h * h_cols // LANES, (h + 1) * h_cols // LANES):
            here = slice(k * LANES, (k + 1) * LANES)
            m, s = m_cols[:, here], s_cols[:, here]
            peak = jnp.max(m, axis=0, keepdims=True)
            total = jnp.sum(s * jnp.exp2(m - peak), axis=0, keepdims=True)
            cbuf[t, row, k : k + 1, :] = peak + jnp.log2(total)
        return send_out(cbuf, t, h, row, nr, c_send, c_recv, lambda i: (i, col))

    def take_cols(t, h, copies):
        g = -log_p - take_in(cbuf, t, h, nr, copies)
        if t < ITERS - 1:
            for k in range(h_cols // LANES):
                lane = h * h_cols + k * LANES
                g8[:, lane : lane + LANES] = jnp.broadcast_to(g[k : k + 1, :], (8, LANES))
        else:
            per = pb // LANES
            for b in range(nr // 2):
                block = h * (nr // 2) + b
                g_out[block * per : (block + 1) * per, :] = (
                    g[b * per : (b + 1) * per, :] / kappa1 + pn[block]
                )

    low = jnp.full((8, LANES), LOW, jnp.float32)
    zero = jnp.zeros((8, LANES), jnp.float32)

    def row_pass(h, c):
        def body(i, _):
            spots = [pl.ds(pl.multiple_of(h * h_rows + i * 32 + r * 8, 8), 8) for r in range(4)]
            pair = [(low, zero) if c == 0 else (m_rows[sp, :], s_rows[sp, :]) for sp in spots]
            for k0 in range(c * h_cols // LANES, (c + 1) * h_cols // LANES, 16):
                for r, at_row in enumerate(spots):
                    z = [
                        tile[at_row, k * LANES : (k + 1) * LANES] + g8[:, k * LANES : (k + 1) * LANES]
                        for k in range(k0, k0 + 16)
                    ]
                    pair[r] = online(*pair[r], z)
            for r, at_row in enumerate(spots):
                m_rows[at_row, :], s_rows[at_row, :] = pair[r]
            return 0

        lax.fori_loop(0, h_rows // 32, body, 0, unroll=2)

    def col_pass(h, c):
        side = 4

        def strip(k, _):
            lanes = [
                pl.ds(pl.multiple_of(c * h_cols + (k * side + i) * LANES, LANES), LANES)
                for i in range(side)
            ]

            def body(j, carry):
                spots = [pl.ds(pl.multiple_of(h * h_rows + j * 128 + r * 8, 8), 8) for r in range(16)]
                f = [fb[sp, :] for sp in spots]
                out = []
                for i in range(side):
                    z = [tile[sp, lanes[i]] + f[r] for r, sp in enumerate(spots)]
                    out.append(online(*carry[i], z))
                return tuple(out)

            start = tuple((low, zero) if h == 0 else (m_cols[:, sp], s_cols[:, sp]) for sp in lanes)
            done = lax.fori_loop(0, h_rows // 128, body, start, unroll=2)
            for i in range(side):
                m_cols[:, lanes[i]], s_cols[:, lanes[i]] = done[i]
            return 0

        lax.fori_loop(0, h_cols // (side * LANES), strip, 0)

    prepare(row, p_ref)
    split_q(col, q_ref)
    work(row, col)
    own.wait_recv()
    split_q(sibling, qbuf.at[sibling])
    work(row, sibling)
    for d, c in enumerate(cross, 1):
        c.wait_recv()
        source = lax.rem(col - 2 * d + nc, nc)
        fwd = remote(
            qbuf.at[source], qbuf.at[source], q_send.at[nx + d - 1], q_recv.at[nx + d - 1],
            (row, sibling),
        )
        fwd.start()
        passed.append(fwd)
        if d == 1:
            for r in steps[1]:
                r.wait_recv()
            steps[2] = ring(2)
            for r in steps[2]:
                r.start()
        split_q(source, qbuf.at[source])
        work(row, source)
    for d, c in enumerate(passed, 1):
        c.wait_recv()
        source = lax.rem(sibling - 2 * d + nc, nc)
        split_q(source, qbuf.at[source])
        work(row, source)

    def all_queries(owner):
        prepare(owner, pbuf.at[owner])

        def body(i, _):
            work(owner, i)
            return 0

        lax.fori_loop(0, nc, body, 0)

    for step in range(1, half):
        if step > 1:
            for c in steps[step]:
                c.wait_recv()
            steps[step + 1] = ring(step + 1)
            for c in steps[step + 1]:
                c.start()
        for owner in (at(pos - step), at(pos + step)):
            all_queries(owner)
    for c in steps[half]:
        c.wait_recv()
    owner = at(pos + half)
    prepare(owner, pbuf.at[owner])
    row_copies = []
    for h in range(2):

        def body(i, _):
            work(owner, i)
            return 0

        lax.fori_loop(h * nc // 2, (h + 1) * nc // 2, body, 0)
        row_copies.append(send_rows(0, h))

    for t in range(ITERS):
        if t > 0:
            row_copies = []
            for h in range(2):
                take_cols(t - 1, h, col_copies[h])
                row_pass(0, h)
                if h == 0:
                    row_pass(1, 0)
            row_copies.append(send_rows(t, 0))
            row_pass(1, 1)
            row_copies.append(send_rows(t, 1))
        take_rows(t, 0, row_copies[0])
        col_pass(0, 0)
        col_pass(0, 1)
        take_rows(t, 1, row_copies[1])
        col_copies = []
        for c in range(2):
            col_pass(1, c)
            col_copies.append(send_cols(t, c))
    for h in range(2):
        take_cols(ITERS - 1, h, col_copies[h])

    for c in sent:
        c.wait_send()
    for c in cross + [own] + passed:
        c.wait_send()
    for step in range(1, half + 1):
        for c in steps[step]:
            c.wait_send()


def per_device(nr, nc, queries, passages, mean_cost):
    qb, depth = queries.shape
    pb = passages.shape[0]
    rows, cols = qb * nc, pb * nr
    f32, bf16 = jnp.float32, jnp.bfloat16
    dma = pltpu.SemaphoreType.DMA
    vmem = pl.BlockSpec(memory_space=pltpu.VMEM)
    f, g = pl.pallas_call(
        functools.partial(
            kernel, nr, nc, math.log2(qb * nr * nc), math.log2(pb * nr * nc)
        ),
        out_shape=(
            jax.ShapeDtypeStruct((rows // LANES, LANES), f32),
            jax.ShapeDtypeStruct((cols // LANES, LANES), f32),
        ),
        in_specs=[pl.BlockSpec(memory_space=pltpu.SMEM), vmem, vmem],
        out_specs=(vmem, vmem),
        scratch_shapes=[
            pltpu.VMEM((rows, cols), f32),
            pltpu.VMEM((nc, qb, depth), f32),
            pltpu.VMEM((nr, pb, depth), f32),
            pltpu.VMEM((rows, 3 * depth), bf16),
            pltpu.VMEM((pb, 3 * depth), bf16),
            pltpu.VMEM((nc, qb // LANES, LANES), f32),
            pltpu.VMEM((nr, pb // LANES, LANES), f32),
            pltpu.VMEM((8, cols), f32),
            pltpu.VMEM((rows, LANES), f32),
            pltpu.VMEM((rows, LANES), f32),
            pltpu.VMEM((rows, LANES), f32),
            pltpu.VMEM((8, cols), f32),
            pltpu.VMEM((8, cols), f32),
            pltpu.VMEM((ITERS, nc, rows // LANES, LANES), f32),
            pltpu.VMEM((ITERS, nr, cols // LANES, LANES), f32),
            dma((nc,)), dma((nc,)),
            dma((2, nr // 2 + 1)), dma((2, nr // 2 + 1)),
            dma((ITERS, 2, nc)), dma((ITERS, 2, nc)),
            dma((ITERS, 2, nr)), dma((ITERS, 2, nr)),
        ],
        compiler_params=pltpu.CompilerParams(
            collective_id=0, has_side_effects=True, vmem_limit_bytes=60 * 1024 * 1024
        ),
        cost_estimate=pl.CostEstimate(
            flops=6 * rows * cols * depth,
            bytes_accessed=4 * depth * (qb + pb),
            transcendentals=2 * ITERS * rows * cols,
        ),
    )(mean_cost, queries, passages)
    return f.reshape(rows), g.reshape(cols)


def solution(mesh):
    nr, nc = mesh.shape["row"], mesh.shape["col"]
    placed = (P(("row", "col"), None), P(("col", "row"), None), P())
    return jax.shard_map(
        functools.partial(per_device, nr, nc),
        mesh=mesh, in_specs=placed, out_specs=(P("row"), P("col")), check_vma=False,
    )
```

```python
import functools
import math

import jax
import jax.numpy as jnp
from jax import lax
from jax.experimental import pallas as pl
from jax.experimental.pallas import tpu as pltpu
from jax.sharding import PartitionSpec as P

ITERS = 3
LOG2E = 1.4426950408889634
LOW = -3.0e38
LANES = 128
MESH = pl.DeviceIdType.MESH


def tree(op, values):
    values = list(values)
    while len(values) > 1:
        values = [
            op(values[i], values[i + 1]) if i + 1 < len(values) else values[i]
            for i in range(0, len(values), 2)
        ]
    return values[0]


def online(m, s, z):
    new = jnp.maximum(m, tree(jnp.maximum, z))
    return new, s * jnp.exp2(m - new) + tree(jnp.add, [jnp.exp2(v - new) for v in z])


def kernel(
    nr, nc, log_q, log_p,
    mc_ref, q_ref, p_ref, f_out, g_out,
    tile, qbuf, pbuf, q3, p3, qn, pn, g8, fb, m_rows, s_rows, m_cols, s_cols, rbuf, cbuf,
    q_send, q_recv, p_send, p_recv, r_send, r_recv, c_send, c_recv,
):
    row, col = lax.axis_index("row"), lax.axis_index("col")
    qb, depth = q_ref.shape
    pb = p_ref.shape[0]
    rows, cols = qb * nc, pb * nr
    nx = nc // 2
    core = lax.rem(col, 2)
    sibling = col + 1 - 2 * core

    barrier = pltpu.get_barrier_semaphore()
    for d in range(1, nr):
        pl.semaphore_signal(
            barrier, inc=1, device_id=(lax.rem(row + d, nr), col), device_id_type=MESH
        )
    for d in range(1, nc):
        pl.semaphore_signal(
            barrier, inc=1, device_id=(row, lax.rem(col + d, nc)), device_id_type=MESH
        )
    pl.semaphore_wait(barrier, nr + nc - 2)

    def remote(src, dst, send, recv, device):
        return pltpu.make_async_remote_copy(
            src_ref=src, dst_ref=dst, send_sem=send, recv_sem=recv,
            device_id=device, device_id_type=MESH,
        )

    half = nr // 2

    def at(pos):
        pos = lax.rem(pos + 2 * nr, nr)
        y = pos // half
        z = pos * (1 - y) + (nr - 1 - pos) * y
        return 2 * z + y

    row_y = lax.rem(row, 2)
    row_z = row // 2
    pos = row_z + row_y * (nr - 1 - 2 * row_z)
    ahead, behind = at(pos + 1), at(pos - 1)

    hb = pb // 2

    def ring(step, turn):
        out = []
        for way, device in enumerate((ahead, behind)):
            owner = at(pos + (step - 1) * (2 * way - 1))
            part = pl.ds((way + turn) % 2 * hb, hb)
            src = p_ref.at[part] if step == 1 else pbuf.at[owner, part]
            c = remote(
                src, pbuf.at[owner, part],
                p_send.at[way, step, turn], p_recv.at[way, step, turn], (device, col),
            )
            c.start()
            out.append(c)
        return out

    steps = {}
    for turn in range(2):
        steps[1, turn] = ring(1, turn)

    def pass_on(step, turn):
        for c in steps[step, turn]:
            c.wait_recv()
        if step + 1 < half or (step + 1 == half and turn == 0):
            steps[step + 1, turn] = ring(step + 1, turn)

    cross, passed = [], []
    for d in range(1, nx):
        cross.append(
            remote(
                q_ref, qbuf.at[col], q_send.at[d], q_recv.at[d],
                (row, lax.rem(col + 2 * d, nc)),
            )
        )
    for c in cross:
        c.start()
    own = remote(q_ref, qbuf.at[col], q_send.at[0], q_recv.at[0], (row, sibling))
    own.start()

    kappa = (10.0 * LOG2E) / jnp.full((8, LANES), mc_ref[0], jnp.float32)
    kappa1 = kappa[0:1, :]

    def norms(x):
        sq = x * x
        total = sq[:, 0:LANES]
        for k in range(1, depth // LANES):
            total = total + sq[:, k * LANES : (k + 1) * LANES]
        return jnp.sum(total.T, axis=0, keepdims=True)

    def split_q(block, ref):
        def body(i, _):
            x = ref[pl.ds(pl.multiple_of(i * LANES, LANES), LANES), :]
            qn[block, pl.ds(i, 1), :] = norms(x)
            for k in range(depth // LANES):
                v = x[:, k * LANES : (k + 1) * LANES] * (2.0 * kappa1)
                hi = v.astype(jnp.bfloat16)
                lo = (v - hi.astype(jnp.float32)).astype(jnp.bfloat16)
                at_row = pl.ds(pl.multiple_of(block * qb + i * LANES, LANES), LANES)
                q3[at_row, k * LANES : (k + 1) * LANES] = hi
                q3[at_row, depth + k * LANES : depth + (k + 1) * LANES] = hi
                q3[at_row, 2 * depth + k * LANES : 2 * depth + (k + 1) * LANES] = lo
            return 0

        lax.fori_loop(0, qb // LANES, body, 0)

    m_rows[...] = jnp.full(m_rows.shape, LOW, jnp.float32)
    s_rows[...] = jnp.zeros(s_rows.shape, jnp.float32)

    def prepare(halves):
        for u, (block, ref, part) in enumerate(halves):
            base = pl.multiple_of(block * pb + part * hb, LANES)
            for i in range(hb // LANES):
                x = ref[part * hb + i * LANES : part * hb + (i + 1) * LANES, :]
                norm = norms(x)
                lane = part * hb // LANES + i
                pn[block, lane : lane + 1, :] = norm
                g8[:, pl.ds(pl.multiple_of(base + i * LANES, LANES), LANES)] = jnp.broadcast_to(
                    -norm * kappa1, (8, LANES)
                )
                hi = x.astype(jnp.bfloat16)
                lo = (x - hi.astype(jnp.float32)).astype(jnp.bfloat16)
                here = slice(u * hb + i * LANES, u * hb + (i + 1) * LANES)
                p3[here, 0:depth] = hi
                p3[here, depth : 2 * depth] = lo
                p3[here, 2 * depth : 3 * depth] = hi

    def work(halves, q_block):
        top = pl.multiple_of(q_block * qb, qb)
        bases = [pl.multiple_of(block * pb + part * hb, LANES) for block, _, part in halves]
        lanes = [
            pl.ds(pl.multiple_of(base + k * LANES, LANES), LANES)
            for base in bases
            for k in range(hb // LANES)
        ]
        product = lax.dot_general(
            q3[pl.ds(top, qb), :], p3[...], (((1,), (1,)), ((), ())),
            preferred_element_type=jnp.float32,
        )
        for u, base in enumerate(bases):
            tile[pl.ds(top, qb), pl.ds(base, hb)] = product[:, u * hb : (u + 1) * hb]

        def first(i, _):
            g = [g8[:, lane] for lane in lanes]
            for r in range(16):
                at_row = pl.ds(pl.multiple_of(top + i * 128 + r * 8, 8), 8)
                z = [tile[at_row, lane] + g[k] for k, lane in enumerate(lanes)]
                m_rows[at_row, :], s_rows[at_row, :] = online(m_rows[at_row, :], s_rows[at_row, :], z)
            return 0

        lax.fori_loop(0, qb // 128, first, 0)

    sent = []

    def send_out(buf, t, h, me, n, send, recv, device):
        size = buf.shape[2] // 2
        half_part = buf.at[t, me, pl.ds(h * size, size)]
        copies = []
        for d in range(1, n):
            c = remote(
                half_part, half_part, send.at[t, h, d], recv.at[t, h, d], device(lax.rem(me + d, n))
            )
            c.start()
            copies.append(c)
        sent.extend(copies)
        return copies

    def take_in(buf, t, h, n, copies):
        for c in copies:
            c.wait_recv()
        size = buf.shape[2] // 2
        parts = [buf[t, i, h * size : (h + 1) * size, :] for i in range(n)]
        peak = tree(jnp.maximum, parts)
        total = jnp.exp2(parts[0] - peak)
        for part in parts[1:]:
            total = total + jnp.exp2(part - peak)
        return peak + jnp.log2(total)

    h_rows, h_cols = rows // 2, cols // 2

    def send_rows(t, h):
        for b in range(h * h_rows // LANES, (h + 1) * h_rows // LANES):
            here = slice(b * LANES, (b + 1) * LANES)
            m, s = m_rows[here, :].T, s_rows[here, :].T
            peak = jnp.max(m, axis=0, keepdims=True)
            total = jnp.sum(s * jnp.exp2(m - peak), axis=0, keepdims=True)
            rbuf[t, col, b : b + 1, :] = peak + jnp.log2(total)
        return send_out(rbuf, t, h, col, nc, r_send, r_recv, lambda i: (row, i))

    def take_rows(t, h, copies):
        f = -log_q - take_in(rbuf, t, h, nc, copies)
        for b in range(h_rows // LANES):
            at_row = h * h_rows + b * LANES
            fb[at_row : at_row + LANES, :] = jnp.broadcast_to(f[b : b + 1, :], (LANES, LANES)).T
        if t == ITERS - 1:
            per = qb // LANES
            for b in range(nc // 2):
                block = h * (nc // 2) + b
                f_out[block * per : (block + 1) * per, :] = (
                    f[b * per : (b + 1) * per, :] / kappa1 + qn[block]
                )

    def send_cols(t, h):
        for k in range(h * h_cols // LANES, (h + 1) * h_cols // LANES):
            here = slice(k * LANES, (k + 1) * LANES)
            m, s = m_cols[:, here], s_cols[:, here]
            peak = jnp.max(m, axis=0, keepdims=True)
            total = jnp.sum(s * jnp.exp2(m - peak), axis=0, keepdims=True)
            cbuf[t, row, k : k + 1, :] = peak + jnp.log2(total)
        return send_out(cbuf, t, h, row, nr, c_send, c_recv, lambda i: (i, col))

    def take_cols(t, h, copies):
        g = -log_p - take_in(cbuf, t, h, nr, copies)
        if t < ITERS - 1:
            for k in range(h_cols // LANES):
                lane = h * h_cols + k * LANES
                g8[:, lane : lane + LANES] = jnp.broadcast_to(g[k : k + 1, :], (8, LANES))
        else:
            per = pb // LANES
            for b in range(nr // 2):
                block = h * (nr // 2) + b
                g_out[block * per : (block + 1) * per, :] = (
                    g[b * per : (b + 1) * per, :] / kappa1 + pn[block]
                )

    low = jnp.full((8, LANES), LOW, jnp.float32)
    zero = jnp.zeros((8, LANES), jnp.float32)

    def row_pass(h, c):
        def body(i, _):
            spots = [pl.ds(pl.multiple_of(h * h_rows + i * 32 + r * 8, 8), 8) for r in range(4)]
            pair = [(low, zero) if c == 0 else (m_rows[sp, :], s_rows[sp, :]) for sp in spots]
            for k0 in range(c * h_cols // LANES, (c + 1) * h_cols // LANES, 16):
                for r, at_row in enumerate(spots):
                    z = [
                        tile[at_row, k * LANES : (k + 1) * LANES] + g8[:, k * LANES : (k + 1) * LANES]
                        for k in range(k0, k0 + 16)
                    ]
                    pair[r] = online(*pair[r], z)
            for r, at_row in enumerate(spots):
                m_rows[at_row, :], s_rows[at_row, :] = pair[r]
            return 0

        lax.fori_loop(0, h_rows // 32, body, 0, unroll=2)

    def col_pass(h, c):
        side = 4

        def strip(k, _):
            lanes = [
                pl.ds(pl.multiple_of(c * h_cols + (k * side + i) * LANES, LANES), LANES)
                for i in range(side)
            ]

            def body(j, carry):
                spots = [pl.ds(pl.multiple_of(h * h_rows + j * 128 + r * 8, 8), 8) for r in range(16)]
                f = [fb[sp, :] for sp in spots]
                out = []
                for i in range(side):
                    z = [tile[sp, lanes[i]] + f[r] for r, sp in enumerate(spots)]
                    out.append(online(*carry[i], z))
                return tuple(out)

            start = tuple((low, zero) if h == 0 else (m_cols[:, sp], s_cols[:, sp]) for sp in lanes)
            done = lax.fori_loop(0, h_rows // 128, body, start, unroll=2)
            for i in range(side):
                m_cols[:, lanes[i]], s_cols[:, lanes[i]] = done[i]
            return 0

        lax.fori_loop(0, h_cols // (side * LANES), strip, 0)

    mine = [(row, p_ref, 0), (row, p_ref, 1)]
    prepare(mine)
    split_q(col, q_ref)
    work(mine, col)
    own.wait_recv()
    split_q(sibling, qbuf.at[sibling])
    work(mine, sibling)
    pass_on(1, 0)
    for d, c in enumerate(cross, 1):
        c.wait_recv()
        source = lax.rem(col - 2 * d + nc, nc)
        fwd = remote(
            qbuf.at[source], qbuf.at[source], q_send.at[nx + d - 1], q_recv.at[nx + d - 1],
            (row, sibling),
        )
        fwd.start()
        passed.append(fwd)
        split_q(source, qbuf.at[source])
        work(mine, source)
    pass_on(1, 1)
    for d, c in enumerate(passed, 1):
        c.wait_recv()
        source = lax.rem(sibling - 2 * d + nc, nc)
        split_q(source, qbuf.at[source])
        work(mine, source)

    def some_queries(halves, start, end):
        def body(i, _):
            work(halves, i)
            return 0

        lax.fori_loop(start, end, body, 0)

    for step in range(1, half):
        for turn in range(2):
            if step > 1:
                pass_on(step, turn)
            left, right = at(pos - step), at(pos + step)
            halves = [(left, pbuf.at[left], turn), (right, pbuf.at[right], 1 - turn)]
            prepare(halves)
            some_queries(halves, 0, nc)
    for c in steps[half, 0]:
        c.wait_recv()
    last = at(pos + half)
    halves = [(last, pbuf.at[last], 0), (last, pbuf.at[last], 1)]
    prepare(halves)
    row_copies = []
    for h in range(2):
        some_queries(halves, h * nc // 2, (h + 1) * nc // 2)
        row_copies.append(send_rows(0, h))

    for t in range(ITERS):
        if t > 0:
            row_copies = []
            for h in range(2):
                take_cols(t - 1, h, col_copies[h])
                row_pass(0, h)
                if h == 0:
                    row_pass(1, 0)
            row_copies.append(send_rows(t, 0))
            row_pass(1, 1)
            row_copies.append(send_rows(t, 1))
        take_rows(t, 0, row_copies[0])
        col_pass(0, 0)
        col_pass(0, 1)
        take_rows(t, 1, row_copies[1])
        col_copies = []
        for c in range(2):
            col_pass(1, c)
            col_copies.append(send_cols(t, c))
    for h in range(2):
        take_cols(ITERS - 1, h, col_copies[h])

    for c in sent:
        c.wait_send()
    for c in cross + [own] + passed:
        c.wait_send()
    for copies in steps.values():
        for c in copies:
            c.wait_send()


def per_device(nr, nc, queries, passages, mean_cost):
    qb, depth = queries.shape
    pb = passages.shape[0]
    rows, cols = qb * nc, pb * nr
    f32, bf16 = jnp.float32, jnp.bfloat16
    dma = pltpu.SemaphoreType.DMA
    vmem = pl.BlockSpec(memory_space=pltpu.VMEM)
    f, g = pl.pallas_call(
        functools.partial(
            kernel, nr, nc, math.log2(qb * nr * nc), math.log2(pb * nr * nc)
        ),
        out_shape=(
            jax.ShapeDtypeStruct((rows // LANES, LANES), f32),
            jax.ShapeDtypeStruct((cols // LANES, LANES), f32),
        ),
        in_specs=[pl.BlockSpec(memory_space=pltpu.SMEM), vmem, vmem],
        out_specs=(vmem, vmem),
        scratch_shapes=[
            pltpu.VMEM((rows, cols), f32),
            pltpu.VMEM((nc, qb, depth), f32),
            pltpu.VMEM((nr, pb, depth), f32),
            pltpu.VMEM((rows, 3 * depth), bf16),
            pltpu.VMEM((pb, 3 * depth), bf16),
            pltpu.VMEM((nc, qb // LANES, LANES), f32),
            pltpu.VMEM((nr, pb // LANES, LANES), f32),
            pltpu.VMEM((8, cols), f32),
            pltpu.VMEM((rows, LANES), f32),
            pltpu.VMEM((rows, LANES), f32),
            pltpu.VMEM((rows, LANES), f32),
            pltpu.VMEM((8, cols), f32),
            pltpu.VMEM((8, cols), f32),
            pltpu.VMEM((ITERS, nc, rows // LANES, LANES), f32),
            pltpu.VMEM((ITERS, nr, cols // LANES, LANES), f32),
            dma((nc,)), dma((nc,)),
            dma((2, nr // 2 + 1, 2)), dma((2, nr // 2 + 1, 2)),
            dma((ITERS, 2, nc)), dma((ITERS, 2, nc)),
            dma((ITERS, 2, nr)), dma((ITERS, 2, nr)),
        ],
        compiler_params=pltpu.CompilerParams(
            collective_id=0, has_side_effects=True, vmem_limit_bytes=60 * 1024 * 1024
        ),
        cost_estimate=pl.CostEstimate(
            flops=6 * rows * cols * depth,
            bytes_accessed=4 * depth * (qb + pb),
            transcendentals=2 * ITERS * rows * cols,
        ),
    )(mean_cost, queries, passages)
    return f.reshape(rows), g.reshape(cols)


def solution(mesh):
    nr, nc = mesh.shape["row"], mesh.shape["col"]
    placed = (P(("row", "col"), None), P(("col", "row"), None), P())
    return jax.shard_map(
        functools.partial(per_device, nr, nc),
        mesh=mesh, in_specs=placed, out_specs=(P("row"), P("col")), check_vma=False,
    )
```

```python
import functools
import math

import jax
import jax.numpy as jnp
from jax import lax
from jax.experimental import pallas as pl
from jax.experimental.pallas import tpu as pltpu
from jax.sharding import PartitionSpec as P

ITERS = 3
LOG2E = 1.4426950408889634
LOW = -3.0e38
LANES = 128
MESH = pl.DeviceIdType.MESH


def tree(op, values):
    values = list(values)
    while len(values) > 1:
        values = [
            op(values[i], values[i + 1]) if i + 1 < len(values) else values[i]
            for i in range(0, len(values), 2)
        ]
    return values[0]


def online(m, s, z):
    new = jnp.maximum(m, tree(jnp.maximum, z))
    return new, s * jnp.exp2(m - new) + tree(jnp.add, [jnp.exp2(v - new) for v in z])


def kernel(
    nr, nc, log_q, log_p,
    mc_ref, q_ref, p_ref, f_out, g_out,
    tile, qbuf, pbuf, q3, p3, qn, pn, g8, fb, m_rows, s_rows, m_cols, s_cols, rbuf, cbuf,
    q_send, q_recv, p_send, p_recv, r_send, r_recv, c_send, c_recv,
):
    row, col = lax.axis_index("row"), lax.axis_index("col")
    qb, depth = q_ref.shape
    pb = p_ref.shape[0]
    rows, cols = qb * nc, pb * nr
    nx = nc // 2
    core = lax.rem(col, 2)
    sibling = col + 1 - 2 * core

    barrier = pltpu.get_barrier_semaphore()
    for d in range(1, nr):
        pl.semaphore_signal(
            barrier, inc=1, device_id=(lax.rem(row + d, nr), col), device_id_type=MESH
        )
    for d in range(1, nc):
        pl.semaphore_signal(
            barrier, inc=1, device_id=(row, lax.rem(col + d, nc)), device_id_type=MESH
        )
    pl.semaphore_wait(barrier, nr + nc - 2)

    def remote(src, dst, send, recv, device):
        return pltpu.make_async_remote_copy(
            src_ref=src, dst_ref=dst, send_sem=send, recv_sem=recv,
            device_id=device, device_id_type=MESH,
        )

    half = nr // 2

    def at(pos):
        pos = lax.rem(pos + 2 * nr, nr)
        y = pos // half
        z = pos * (1 - y) + (nr - 1 - pos) * y
        return 2 * z + y

    row_y = lax.rem(row, 2)
    row_z = row // 2
    pos = row_z + row_y * (nr - 1 - 2 * row_z)
    ahead, behind = at(pos + 1), at(pos - 1)

    hb = pb // 2

    def ring(step, turn):
        out = []
        for way, device in enumerate((ahead, behind)):
            owner = at(pos + (step - 1) * (2 * way - 1))
            part = pl.ds((way + turn) % 2 * hb, hb)
            src = p_ref.at[part] if step == 1 else pbuf.at[owner, part]
            c = remote(
                src, pbuf.at[owner, part],
                p_send.at[way, step, turn], p_recv.at[way, step, turn], (device, col),
            )
            c.start()
            out.append(c)
        return out

    steps = {}
    for turn in range(2):
        steps[1, turn] = ring(1, turn)

    def pass_on(step, turn):
        for c in steps[step, turn]:
            c.wait_recv()
        if step + 1 < half or (step + 1 == half and turn == 0):
            steps[step + 1, turn] = ring(step + 1, turn)

    cross, passed = [], []
    for d in range(1, nx):
        cross.append(
            remote(
                q_ref, qbuf.at[col], q_send.at[d], q_recv.at[d],
                (row, lax.rem(col + 2 * d, nc)),
            )
        )
    for c in cross:
        c.start()
    own = remote(q_ref, qbuf.at[col], q_send.at[0], q_recv.at[0], (row, sibling))
    own.start()

    kappa = (10.0 * LOG2E) / jnp.full((8, LANES), mc_ref[0], jnp.float32)
    kappa1 = kappa[0:1, :]

    def norms(x):
        sq = x * x
        total = sq[:, 0:LANES]
        for k in range(1, depth // LANES):
            total = total + sq[:, k * LANES : (k + 1) * LANES]
        return jnp.sum(total.T, axis=0, keepdims=True)

    def split_q(block, ref):
        def body(i, _):
            x = ref[pl.ds(pl.multiple_of(i * LANES, LANES), LANES), :]
            qn[block, pl.ds(i, 1), :] = norms(x)
            for k in range(depth // LANES):
                v = x[:, k * LANES : (k + 1) * LANES] * (2.0 * kappa1)
                hi = v.astype(jnp.bfloat16)
                lo = (v - hi.astype(jnp.float32)).astype(jnp.bfloat16)
                at_row = pl.ds(pl.multiple_of(block * qb + i * LANES, LANES), LANES)
                q3[at_row, k * LANES : (k + 1) * LANES] = hi
                q3[at_row, depth + k * LANES : depth + (k + 1) * LANES] = hi
                q3[at_row, 2 * depth + k * LANES : 2 * depth + (k + 1) * LANES] = lo
            return 0

        lax.fori_loop(0, qb // LANES, body, 0)

    m_rows[...] = jnp.full(m_rows.shape, LOW, jnp.float32)
    s_rows[...] = jnp.zeros(s_rows.shape, jnp.float32)

    def prepare(halves):
        for u, (block, ref, part) in enumerate(halves):
            base = pl.multiple_of(block * pb + part * hb, LANES)
            for i in range(hb // LANES):
                x = ref[part * hb + i * LANES : part * hb + (i + 1) * LANES, :]
                norm = norms(x)
                lane = part * hb // LANES + i
                pn[block, lane : lane + 1, :] = norm
                g8[:, pl.ds(pl.multiple_of(base + i * LANES, LANES), LANES)] = jnp.broadcast_to(
                    -norm * kappa1, (8, LANES)
                )
                here = slice(u * hb + i * LANES, u * hb + (i + 1) * LANES)
                for k in range(depth // LANES):
                    v = x[:, k * LANES : (k + 1) * LANES].T
                    hi = v.astype(jnp.bfloat16)
                    lo = (v - hi.astype(jnp.float32)).astype(jnp.bfloat16)
                    for piece, value in enumerate((hi, lo, hi)):
                        spot = piece * depth + k * LANES
                        p3[spot : spot + LANES, here] = value

    def work(halves, q_block):
        top = pl.multiple_of(q_block * qb, qb)
        bases = [pl.multiple_of(block * pb + part * hb, LANES) for block, _, part in halves]
        lanes = [
            pl.ds(pl.multiple_of(base + k * LANES, LANES), LANES)
            for base in bases
            for k in range(hb // LANES)
        ]
        product = lax.dot_general(
            q3[pl.ds(top, qb), :], p3[...], (((1,), (0,)), ((), ())),
            preferred_element_type=jnp.float32,
        )
        for u, base in enumerate(bases):
            tile[pl.ds(top, qb), pl.ds(base, hb)] = product[:, u * hb : (u + 1) * hb]

        def first(i, _):
            g = [g8[:, lane] for lane in lanes]
            for r in range(16):
                at_row = pl.ds(pl.multiple_of(top + i * 128 + r * 8, 8), 8)
                z = [tile[at_row, lane] + g[k] for k, lane in enumerate(lanes)]
                m_rows[at_row, :], s_rows[at_row, :] = online(m_rows[at_row, :], s_rows[at_row, :], z)
            return 0

        lax.fori_loop(0, qb // 128, first, 0)

    sent = []

    def send_out(buf, t, h, me, n, send, recv, device):
        size = buf.shape[2] // 2
        half_part = buf.at[t, me, pl.ds(h * size, size)]
        copies = []
        for d in range(1, n):
            c = remote(
                half_part, half_part, send.at[t, h, d], recv.at[t, h, d], device(lax.rem(me + d, n))
            )
            c.start()
            copies.append(c)
        sent.extend(copies)
        return copies

    def take_in(buf, t, h, n, copies):
        for c in copies:
            c.wait_recv()
        size = buf.shape[2] // 2
        parts = [buf[t, i, h * size : (h + 1) * size, :] for i in range(n)]
        peak = tree(jnp.maximum, parts)
        total = jnp.exp2(parts[0] - peak)
        for part in parts[1:]:
            total = total + jnp.exp2(part - peak)
        return peak + jnp.log2(total)

    h_rows, h_cols = rows // 2, cols // 2

    def send_rows(t, h):
        for b in range(h * h_rows // LANES, (h + 1) * h_rows // LANES):
            here = slice(b * LANES, (b + 1) * LANES)
            m, s = m_rows[here, :].T, s_rows[here, :].T
            peak = jnp.max(m, axis=0, keepdims=True)
            total = jnp.sum(s * jnp.exp2(m - peak), axis=0, keepdims=True)
            rbuf[t, col, b : b + 1, :] = peak + jnp.log2(total)
        return send_out(rbuf, t, h, col, nc, r_send, r_recv, lambda i: (row, i))

    def take_rows(t, h, copies):
        f = -log_q - take_in(rbuf, t, h, nc, copies)
        for b in range(h_rows // LANES):
            at_row = h * h_rows + b * LANES
            fb[at_row : at_row + LANES, :] = jnp.broadcast_to(f[b : b + 1, :], (LANES, LANES)).T
        if t == ITERS - 1:
            per = qb // LANES
            for b in range(nc // 2):
                block = h * (nc // 2) + b
                f_out[block * per : (block + 1) * per, :] = (
                    f[b * per : (b + 1) * per, :] / kappa1 + qn[block]
                )

    def send_cols(t, h):
        for k in range(h * h_cols // LANES, (h + 1) * h_cols // LANES):
            here = slice(k * LANES, (k + 1) * LANES)
            m, s = m_cols[:, here], s_cols[:, here]
            peak = jnp.max(m, axis=0, keepdims=True)
            total = jnp.sum(s * jnp.exp2(m - peak), axis=0, keepdims=True)
            cbuf[t, row, k : k + 1, :] = peak + jnp.log2(total)
        return send_out(cbuf, t, h, row, nr, c_send, c_recv, lambda i: (i, col))

    def take_cols(t, h, copies):
        g = -log_p - take_in(cbuf, t, h, nr, copies)
        if t < ITERS - 1:
            for k in range(h_cols // LANES):
                lane = h * h_cols + k * LANES
                g8[:, lane : lane + LANES] = jnp.broadcast_to(g[k : k + 1, :], (8, LANES))
        else:
            per = pb // LANES
            for b in range(nr // 2):
                block = h * (nr // 2) + b
                g_out[block * per : (block + 1) * per, :] = (
                    g[b * per : (b + 1) * per, :] / kappa1 + pn[block]
                )

    low = jnp.full((8, LANES), LOW, jnp.float32)
    zero = jnp.zeros((8, LANES), jnp.float32)

    def row_pass(h, c):
        def body(i, _):
            spots = [pl.ds(pl.multiple_of(h * h_rows + i * 32 + r * 8, 8), 8) for r in range(4)]
            pair = [(low, zero) if c == 0 else (m_rows[sp, :], s_rows[sp, :]) for sp in spots]
            for k0 in range(c * h_cols // LANES, (c + 1) * h_cols // LANES, 16):
                for r, at_row in enumerate(spots):
                    z = [
                        tile[at_row, k * LANES : (k + 1) * LANES] + g8[:, k * LANES : (k + 1) * LANES]
                        for k in range(k0, k0 + 16)
                    ]
                    pair[r] = online(*pair[r], z)
            for r, at_row in enumerate(spots):
                m_rows[at_row, :], s_rows[at_row, :] = pair[r]
            return 0

        lax.fori_loop(0, h_rows // 32, body, 0, unroll=4)

    def col_pass(h, c):
        side = 4

        def strip(k, _):
            lanes = [
                pl.ds(pl.multiple_of(c * h_cols + (k * side + i) * LANES, LANES), LANES)
                for i in range(side)
            ]

            def body(j, carry):
                spots = [pl.ds(pl.multiple_of(h * h_rows + j * 128 + r * 8, 8), 8) for r in range(16)]
                f = [fb[sp, :] for sp in spots]
                out = []
                for i in range(side):
                    z = [tile[sp, lanes[i]] + f[r] for r, sp in enumerate(spots)]
                    out.append(online(*carry[i], z))
                return tuple(out)

            start = tuple((low, zero) if h == 0 else (m_cols[:, sp], s_cols[:, sp]) for sp in lanes)
            done = lax.fori_loop(0, h_rows // 128, body, start, unroll=4)
            for i in range(side):
                m_cols[:, lanes[i]], s_cols[:, lanes[i]] = done[i]
            return 0

        lax.fori_loop(0, h_cols // (side * LANES), strip, 0)

    mine = [(row, p_ref, 0), (row, p_ref, 1)]
    prepare(mine)
    split_q(col, q_ref)
    work(mine, col)
    own.wait_recv()
    split_q(sibling, qbuf.at[sibling])
    work(mine, sibling)
    pass_on(1, 0)
    for d, c in enumerate(cross, 1):
        c.wait_recv()
        source = lax.rem(col - 2 * d + nc, nc)
        fwd = remote(
            qbuf.at[source], qbuf.at[source], q_send.at[nx + d - 1], q_recv.at[nx + d - 1],
            (row, sibling),
        )
        fwd.start()
        passed.append(fwd)
        split_q(source, qbuf.at[source])
        work(mine, source)
    pass_on(1, 1)
    for d, c in enumerate(passed, 1):
        c.wait_recv()
        source = lax.rem(sibling - 2 * d + nc, nc)
        split_q(source, qbuf.at[source])
        work(mine, source)

    def some_queries(halves, start, end):
        def body(i, _):
            work(halves, i)
            return 0

        lax.fori_loop(start, end, body, 0)

    for step in range(1, half):
        for turn in range(2):
            if step > 1:
                pass_on(step, turn)
            left, right = at(pos - step), at(pos + step)
            halves = [(left, pbuf.at[left], turn), (right, pbuf.at[right], 1 - turn)]
            prepare(halves)
            some_queries(halves, 0, nc)
    for c in steps[half, 0]:
        c.wait_recv()
    last = at(pos + half)
    halves = [(last, pbuf.at[last], 0), (last, pbuf.at[last], 1)]
    prepare(halves)
    row_copies = []
    for h in range(2):
        some_queries(halves, h * nc // 2, (h + 1) * nc // 2)
        row_copies.append(send_rows(0, h))

    for t in range(ITERS):
        if t > 0:
            row_copies = []
            for h in range(2):
                take_cols(t - 1, h, col_copies[h])
                row_pass(0, h)
                if h == 0:
                    row_pass(1, 0)
            row_copies.append(send_rows(t, 0))
            row_pass(1, 1)
            row_copies.append(send_rows(t, 1))
        take_rows(t, 0, row_copies[0])
        col_pass(0, 0)
        col_pass(0, 1)
        take_rows(t, 1, row_copies[1])
        col_copies = []
        for c in range(2):
            col_pass(1, c)
            col_copies.append(send_cols(t, c))
    for h in range(2):
        take_cols(ITERS - 1, h, col_copies[h])

    for c in sent:
        c.wait_send()
    for c in cross + [own] + passed:
        c.wait_send()
    for copies in steps.values():
        for c in copies:
            c.wait_send()


def per_device(nr, nc, queries, passages, mean_cost):
    qb, depth = queries.shape
    pb = passages.shape[0]
    rows, cols = qb * nc, pb * nr
    f32, bf16 = jnp.float32, jnp.bfloat16
    dma = pltpu.SemaphoreType.DMA
    vmem = pl.BlockSpec(memory_space=pltpu.VMEM)
    f, g = pl.pallas_call(
        functools.partial(
            kernel, nr, nc, math.log2(qb * nr * nc), math.log2(pb * nr * nc)
        ),
        out_shape=(
            jax.ShapeDtypeStruct((rows // LANES, LANES), f32),
            jax.ShapeDtypeStruct((cols // LANES, LANES), f32),
        ),
        in_specs=[pl.BlockSpec(memory_space=pltpu.SMEM), vmem, vmem],
        out_specs=(vmem, vmem),
        scratch_shapes=[
            pltpu.VMEM((rows, cols), f32),
            pltpu.VMEM((nc, qb, depth), f32),
            pltpu.VMEM((nr, pb, depth), f32),
            pltpu.VMEM((rows, 3 * depth), bf16),
            pltpu.VMEM((3 * depth, pb), bf16),
            pltpu.VMEM((nc, qb // LANES, LANES), f32),
            pltpu.VMEM((nr, pb // LANES, LANES), f32),
            pltpu.VMEM((8, cols), f32),
            pltpu.VMEM((rows, LANES), f32),
            pltpu.VMEM((rows, LANES), f32),
            pltpu.VMEM((rows, LANES), f32),
            pltpu.VMEM((8, cols), f32),
            pltpu.VMEM((8, cols), f32),
            pltpu.VMEM((ITERS, nc, rows // LANES, LANES), f32),
            pltpu.VMEM((ITERS, nr, cols // LANES, LANES), f32),
            dma((nc,)), dma((nc,)),
            dma((2, nr // 2 + 1, 2)), dma((2, nr // 2 + 1, 2)),
            dma((ITERS, 2, nc)), dma((ITERS, 2, nc)),
            dma((ITERS, 2, nr)), dma((ITERS, 2, nr)),
        ],
        compiler_params=pltpu.CompilerParams(
            collective_id=0, has_side_effects=True, vmem_limit_bytes=60 * 1024 * 1024
        ),
        cost_estimate=pl.CostEstimate(
            flops=6 * rows * cols * depth,
            bytes_accessed=4 * depth * (qb + pb),
            transcendentals=2 * ITERS * rows * cols,
        ),
    )(mean_cost, queries, passages)
    return f.reshape(rows), g.reshape(cols)


def solution(mesh):
    nr, nc = mesh.shape["row"], mesh.shape["col"]
    placed = (P(("row", "col"), None), P(("col", "row"), None), P())
    return jax.shard_map(
        functools.partial(per_device, nr, nc),
        mesh=mesh, in_specs=placed, out_specs=(P("row"), P("col")), check_vma=False,
    )
```
